32 devices in a mesh: groups: 2 (over y), row: 8 (over z, core), col: 2 (over x).
Axes of the slice: x: 2, y: 2, z: 4, core: 2. Of those that a mesh axis runs over, the one named last changes fastest.
Arguments:
- homolog_features: bfloat16 [32, 256, 256], P(('groups', 'row'), 'col'), parts along dimension 0, may hold values from -6 to 6
- couple_features: bfloat16 [512, 256, 128], P(('groups', 'col'), 'row'), parts along dimension 0, may hold values from -6 to 6
- strand_start_amino: int32 [8], P('groups'), parts along dimension 0, may hold values from 0 to 192, as said below
- homolog_strand_label: int32 [32], P('groups'), parts along dimension 0, may hold values from 0 to 4, as said below
- tensor_product_source: bfloat16 [256, 32], replicated, may hold values from -0.375 to 0.375
- tensor_product_target: bfloat16 [256, 32], replicated, may hold values from -0.375 to 0.375
- tensor_product_final: bfloat16 [1024, 128], replicated, may hold values from -1 to 1
- couple_offset_tensor: float32 [128, 8], replicated
- probe_tensor: bfloat16 [256, 256], replicated, may hold values from -0.375 to 0.375
- lookup_content_tensor: bfloat16 [256, 512], replicated, may hold values from -0.375 to 0.375
- sigmoid_factor_tensor: bfloat16 [256, 256], replicated, may hold values from -0.375 to 0.375
- heads_merge_tensor: bfloat16 [256, 256], replicated, may hold values from -0.75 to 0.75
Outputs:
- refreshed_homologs: bfloat16 [32, 256, 256], P(('groups', 'row'), 'col'), parts along dimension 0
- pair_output_state: bfloat16 [512, 256, 128], P(('groups', 'col'), 'row'), parts along dimension 0
The draws below stay inside these ranges and needn't reach their ends.
There are 2 independent parts, one for each index of `groups`. The reference program is written for one: setup_inputs(seed, part) draws one part's arguments, and reference() takes and returns one part's arrays. A program takes and returns all parts, laid end to end along the dimension named above; an argument that names none is the same for every part. Nothing has to cross between parts.
Inputs may be any that keep to these rules, and one draw needn't show every extreme that they name: `strand_start_amino`: strictly increasing with first entry 0 and last entry 192; chain k holds residues from entry k up to the next entry, the last chain up to 255. `homolog_strand_label`: a row with value 4 is paired and covers all residues; a row with value k covers chain k only; at least 8 rows are paired and every chain has a row of its own.
All inputs are finite; a program needn't handle non-finite values.
Results may differ from the reference program's by a relative error of at most 0.025.
The reference program's roundings to bfloat16 on the way count: a program that leaves them out, or rounds other values in their place, can miss the bound.
Values may be sent and summed in bfloat16 or wider, within the bound.
A program may use at most 128 MiB of HBM per device.

```python
import math
import jax
import jax.numpy as jnp
from jax import lax

FEATURE_BREADTH = 256
CZ = 128
PRODUCT_WIDTH = 32
HEAD_TOTAL = 8
HEAD_BREADTH = 32
CHAINS = 4
AMINO_TOTAL = 256
HOMOLOG_TOTAL = 16


def draw_strand_start_amino(key, part):
    key = jax.random.fold_in(key, 11)
    last_start = AMINO_TOTAL - AMINO_TOTAL // 4
    order = jax.random.permutation(key, last_start - 1).astype(jnp.int32)
    picked = jnp.sort(order[:CHAINS - 2]) + 1
    return jnp.concatenate([jnp.zeros((1,), jnp.int32), picked.astype(jnp.int32), jnp.full((1,), last_start, jnp.int32)])


def draw_homolog_strand_label(key, part):
    key = jax.random.fold_in(key, 23)
    order = jax.random.permutation(key, HOMOLOG_TOTAL).astype(jnp.int32)
    return jnp.where(order < HOMOLOG_TOTAL // 2, CHAINS, order % CHAINS).astype(jnp.int32)


def draw_couple_offset_tensor(key, part):
    key = jax.random.fold_in(key, 37)
    first_key, second_key = jax.random.split(key)
    base = jax.random.normal(first_key, (CZ, HEAD_TOTAL), jnp.float32) / math.sqrt(CZ)
    factor = jnp.exp(jax.random.uniform(second_key, (1, HEAD_TOTAL), jnp.float32, math.log(1.0), math.log(6.0)))
    return base * factor


def levels(key, shape, pieces, least, largest):
    level, own = 1.0, jax.random.fold_in(key, 6)
    for axis_at, blocks in pieces:
        steps = jnp.exp(jax.random.uniform(jax.random.fold_in(own, axis_at), (blocks,), jnp.float32, least / len(pieces), largest / len(pieces)))
        level = level * jnp.repeat(steps, shape[axis_at] // blocks).reshape([-1 if axis == axis_at else 1 for axis in range(len(shape))])
    return level


def gaussian(stream_key, extent, scale, most, cuts=(), kind=jnp.bfloat16):
    values = scale * jax.random.normal(stream_key, extent, jnp.float32)
    if cuts:
        values = values * levels(stream_key, extent, cuts, -0.22, 0.18)
    return jnp.clip(values, -most, most).astype(kind)


def setup_inputs(seed: int = 0, part: int = 0) -> dict:
    arg_keys = jax.random.split(jax.random.key(seed), 13)
    part_splits = jax.random.split(jax.random.fold_in(arg_keys[12], part), 13)
    homolog_features = gaussian(part_splits[0], (HOMOLOG_TOTAL, AMINO_TOTAL, FEATURE_BREADTH), 1.0, 6.0, ((0, 8), (1, 2)))
    couple_features = gaussian(part_splits[1], (AMINO_TOTAL, AMINO_TOTAL, CZ), 1.0, 6.0, ((0, 2), (1, 8)))
    strand_start_amino = draw_strand_start_amino(jax.random.fold_in(jax.random.fold_in(arg_keys[12], part), 71), part)
    homolog_strand_label = draw_homolog_strand_label(jax.random.fold_in(jax.random.fold_in(arg_keys[12], part), 71), part)
    tensor_product_source = gaussian(arg_keys[4], (FEATURE_BREADTH, PRODUCT_WIDTH), FEATURE_BREADTH ** -0.5, 0.375)
    tensor_product_target = gaussian(arg_keys[5], (FEATURE_BREADTH, PRODUCT_WIDTH), FEATURE_BREADTH ** -0.5, 0.375)
    tensor_product_final = gaussian(arg_keys[6], (PRODUCT_WIDTH * PRODUCT_WIDTH, CZ), PRODUCT_WIDTH ** -0.5, 1.0)
    couple_offset_tensor = draw_couple_offset_tensor(jax.random.fold_in(arg_keys[12], 71), part)
    probe_tensor = gaussian(arg_keys[8], (FEATURE_BREADTH, HEAD_TOTAL * HEAD_BREADTH), FEATURE_BREADTH ** -0.5, 0.375)
    lookup_content_tensor = gaussian(arg_keys[9], (FEATURE_BREADTH, 2 * HEAD_TOTAL * HEAD_BREADTH), FEATURE_BREADTH ** -0.5, 0.375)
    sigmoid_factor_tensor = gaussian(arg_keys[10], (FEATURE_BREADTH, HEAD_TOTAL * HEAD_BREADTH), FEATURE_BREADTH ** -0.5, 0.375)
    heads_merge_tensor = gaussian(arg_keys[11], (HEAD_TOTAL * HEAD_BREADTH, FEATURE_BREADTH), (HEAD_TOTAL * HEAD_BREADTH // 4) ** -0.5, 0.75)
    return dict(homolog_features=homolog_features, couple_features=couple_features, strand_start_amino=strand_start_amino, homolog_strand_label=homolog_strand_label, tensor_product_source=tensor_product_source, tensor_product_target=tensor_product_target, tensor_product_final=tensor_product_final, couple_offset_tensor=couple_offset_tensor, probe_tensor=probe_tensor, lookup_content_tensor=lookup_content_tensor, sigmoid_factor_tensor=sigmoid_factor_tensor, heads_merge_tensor=heads_merge_tensor)


EPS = 1e-05

def standardize_features(values):
    values = values.astype(jnp.float32)
    center = values - lax.optimization_barrier(jnp.mean(values, axis=-1, keepdims=True))
    spread = lax.optimization_barrier(jnp.mean(center * center, axis=-1, keepdims=True))
    return center * lax.rsqrt(spread + EPS)

def linear_transform(values, weight):
    flattened = values.reshape(-1, values.shape[-1])
    result = jnp.dot(flattened, weight, preferred_element_type=jnp.float32)
    return result.reshape(values.shape[:-1] + (weight.shape[1],))

def alignment_row_mask(row_chain, position, strand_start_amino):
    chains = strand_start_amino.shape[0]
    owning = lax.optimization_barrier(jnp.sum((position[:, None] >= strand_start_amino[None, :]).astype(jnp.int32), axis=1)) - 1
    kept_entry = (row_chain[:, None] == chains) | (row_chain[:, None] == owning[None, :])
    return kept_entry.astype(jnp.float32)

def outer_update(left_block, right_rows, count_block, pair_block, tensor_product_final):
    collected_homologs, rows_here, width = left_block.shape
    cols_here = right_rows.shape[1]
    left_matrix = left_block.transpose(1, 2, 0).reshape(rows_here * width, collected_homologs)
    right_matrix = right_rows.reshape(collected_homologs, cols_here * width)
    outer = jnp.dot(left_matrix, right_matrix, preferred_element_type=jnp.float32).astype(jnp.bfloat16)
    outer = outer.reshape(rows_here, width, cols_here, width).transpose(0, 2, 1, 3)
    outer = outer.reshape(rows_here * cols_here, width * width)
    update = jnp.dot(outer, tensor_product_final, preferred_element_type=jnp.float32).reshape(rows_here, cols_here, -1)
    return (pair_block.astype(jnp.float32) + update / (count_block[:, :, None] + 0.001)).astype(jnp.bfloat16)

def attend_row(query_row, keyval_row, mask_row, bias_all):
    heads = bias_all.shape[0]
    amino_numbers = query_row.shape[0]
    head_dim = query_row.shape[1] // heads
    inner = heads * head_dim
    queries = query_row.astype(jnp.float32).reshape(amino_numbers, heads, head_dim)
    keys = keyval_row[:, :inner].astype(jnp.float32).reshape(amino_numbers, heads, head_dim)
    vals = keyval_row[:, inner:].astype(jnp.float32).reshape(amino_numbers, heads, head_dim)
    scores = jnp.einsum('ihd,jhd->hij', queries, keys) / math.sqrt(head_dim)
    scores = scores + bias_all.astype(jnp.float32) + ((mask_row - 1.0) * 1000000000.0)[None, None, :]
    peak = lax.optimization_barrier(jnp.max(scores, axis=-1, keepdims=True))
    weights = jnp.exp(scores - peak)
    rounded = weights.astype(jnp.bfloat16).astype(jnp.float32)
    summed = lax.optimization_barrier(jnp.sum(weights, axis=-1))
    attended = jnp.einsum('hij,jhd->ihd', rounded, vals) / summed.T[:, :, None]
    return attended.reshape(amino_numbers, inner)

def reference(homolog_features, couple_features, strand_start_amino, homolog_strand_label, tensor_product_source, tensor_product_target, tensor_product_final, couple_offset_tensor, probe_tensor, lookup_content_tensor, sigmoid_factor_tensor, heads_merge_tensor):
    collected_homologs, amino_numbers = (homolog_features.shape[0], homolog_features.shape[1])
    heads = couple_offset_tensor.shape[1]
    residue_positions = jnp.arange(amino_numbers, dtype=jnp.int32)
    sequence_mask = alignment_row_mask(homolog_strand_label, residue_positions, strand_start_amino)
    standardized_homologs = standardize_features(homolog_features).astype(jnp.bfloat16)
    gathered_left_rows = (linear_transform(standardized_homologs, tensor_product_source) * sequence_mask[:, :, None]).astype(jnp.bfloat16)
    gathered_right_rows = (linear_transform(standardized_homologs, tensor_product_target) * sequence_mask[:, :, None]).astype(jnp.bfloat16)
    count = jnp.dot(sequence_mask.T, sequence_mask, precision=lax.Precision.HIGHEST, preferred_element_type=jnp.float32)
    block = math.gcd(amino_numbers, 16)
    blocks = amino_numbers // block
    left_blocks = gathered_left_rows.reshape(collected_homologs, blocks, block, -1).transpose(1, 0, 2, 3)
    count_blocks = count.reshape(blocks, block, amino_numbers)
    pair_blocks = couple_features.reshape(blocks, block, amino_numbers, -1)

    def one_block(inputs):
        left_block, count_block, pair_block = inputs
        pair_new = outer_update(left_block, gathered_right_rows, count_block, pair_block, tensor_product_final)
        pair_normed = standardize_features(pair_new).astype(jnp.bfloat16)
        bias_new = jnp.dot(pair_normed.reshape(-1, pair_normed.shape[-1]).astype(jnp.float32), couple_offset_tensor, precision=lax.Precision.HIGHEST, preferred_element_type=jnp.float32)
        return (pair_new, bias_new.astype(jnp.bfloat16).reshape(block, amino_numbers, heads))
    pair_parts, bias_parts = lax.map(one_block, (left_blocks, count_blocks, pair_blocks))
    pair_output_state = pair_parts.reshape(amino_numbers, amino_numbers, -1)
    bias_all = bias_parts.reshape(amino_numbers, amino_numbers, heads).transpose(2, 0, 1)
    query_vectors = linear_transform(standardized_homologs, probe_tensor).astype(jnp.bfloat16)
    key_value_pairs = linear_transform(standardized_homologs, lookup_content_tensor).astype(jnp.bfloat16)
    gate_signal = jax.nn.sigmoid(linear_transform(standardized_homologs, sigmoid_factor_tensor))

    def one_row(items):
        query_row, keyval_row, mask_row = items
        return attend_row(query_row, keyval_row, mask_row, bias_all)
    attended = lax.map(one_row, (query_vectors, key_value_pairs, sequence_mask))
    sigmoid_scaled_result = (gate_signal * attended).astype(jnp.bfloat16)
    refreshed_homologs = (homolog_features.astype(jnp.float32) + linear_transform(sigmoid_scaled_result, heads_merge_tensor)).astype(jnp.bfloat16)
    return (refreshed_homologs, pair_output_state)
```

```python
import functools
import math

import jax
import jax.numpy as jnp
from jax import lax
from jax.experimental import pallas as pl
from jax.experimental.pallas import tpu as pltpu
from jax.sharding import PartitionSpec as P

EPS = 1e-05
MESH = pl.DeviceIdType.MESH
F32 = jnp.float32
BF16 = jnp.bfloat16


def standardize(values):
    center = values - jnp.mean(values, axis=-1, keepdims=True)
    spread = jnp.mean(center * center, axis=-1, keepdims=True)
    return center * lax.rsqrt(spread + EPS)


def dot_nt(a, b):
    return lax.dot_general(a, b, (((1,), (1,)), ((), ())), preferred_element_type=F32)


def dot_nn(a, b):
    return jnp.dot(a, b, preferred_element_type=F32)


def transposed(a):
    return a.astype(F32).T.astype(BF16)


def chain_of(position, start_ref, chains):
    chain = (position >= start_ref[0]).astype(jnp.int32)
    for k in range(1, chains):
        chain = chain + (position >= start_ref[k]).astype(jnp.int32)
    return chain - 1


def kernel(
    R, C,
    start_ref, label_ref, x_ref, couple_ref, wsrc_ref, wtgt_ref, wfin_ref, woff_ref,
    wq_ref, wkv_ref, wg_ref, wm_ref,
    out_ref, pair_ref,
    lsend, lall, rsend, rall, xall, lscr, rscr, wd, bscr, cf, biasf, ball,
    qbd, gt, kscr, vt, madd, gated,
    l_send, l_recv, r_send, r_recv, x_send, x_recv, b_send, b_recv, f_send, f_recv,
):
    SL, I, CH = x_ref.shape
    J, Z = couple_ref.shape[1], couple_ref.shape[2]
    S = label_ref.shape[0]
    chains = start_ref.shape[0]
    H = woff_ref.shape[1]
    PW = wsrc_ref.shape[1]
    inner = wq_ref.shape[1]
    D = inner // H
    A = C * I
    Q = I // J
    group = 128 // D
    halves = J // 16
    g = lax.axis_index("groups")
    r = lax.axis_index("row")
    c = lax.axis_index("col")
    n = R * C
    me = r * C + c

    barrier = pltpu.get_barrier_semaphore()

    def greet(k, carry):
        t = lax.rem(me + k, n)
        pl.semaphore_signal(
            barrier, inc=1, device_id=(g, lax.div(t, C), lax.rem(t, C)), device_id_type=MESH
        )
        return carry

    lax.fori_loop(1, n, greet, 0)

    xn = standardize(x_ref[...].astype(F32).reshape(SL * I, CH))
    chain_i = chain_of(
        c * I + lax.broadcasted_iota(jnp.int32, (I, CH), 0), start_ref, chains
    )
    labels = [label_ref[r * SL + s] for s in range(SL)]
    xm = []
    for s in range(SL):
        kept = jnp.logical_or(chain_i == labels[s], labels[s] == chains)
        xm.append(jnp.where(kept, xn[s * I : (s + 1) * I], 0.0).astype(BF16))
    xn = xn.astype(BF16)
    wsrc_t = transposed(wsrc_ref[...])
    for s in range(SL):
        lsend[s] = dot_nt(wsrc_t, xm[s]).astype(BF16)
    wt = wtgt_ref[...].astype(F32)
    wt = jnp.concatenate([wt] * (128 // PW), axis=1)
    wt_lane = lax.broadcasted_iota(jnp.int32, wt.shape, 1) // PW
    packed = None
    for half in range(halves):
        for s in range(SL):
            k = half * SL + s
            rows = xm[s].reshape(Q, halves, 16, CH)[:, half].reshape(Q * 16, CH)
            part = dot_nn(rows, jnp.where(wt_lane == k, wt, 0.0).astype(BF16))
            packed = part if packed is None else packed + part
    rsend[...] = packed.astype(BF16).reshape(Q, 16, 128)

    pl.semaphore_wait(barrier, n - 1)

    def copy_l(k):
        t = lax.rem(r + k, R)
        return pltpu.make_async_remote_copy(
            src_ref=lsend, dst_ref=lall.at[r], send_sem=l_send.at[k], recv_sem=l_recv.at[k],
            device_id=(g, t, c), device_id_type=MESH,
        )

    def copy_r(q, cc):
        return pltpu.make_async_remote_copy(
            src_ref=rsend.at[q], dst_ref=rall.at[r], send_sem=r_send.at[q * C + cc],
            recv_sem=r_recv.at[r], device_id=(g, c * Q + q, cc), device_id_type=MESH,
        )

    def copy_x(k):
        return pltpu.make_async_remote_copy(
            src_ref=x_ref, dst_ref=xall.at[c], send_sem=x_send.at[k], recv_sem=x_recv.at[k],
            device_id=(g, r, lax.rem(c + k, C)), device_id_type=MESH,
        )

    for q in range(Q):
        for cc in range(C):
            @pl.when(jnp.logical_not(jnp.logical_and(c * Q + q == r, cc == c)))
            def _(q=q, cc=cc):
                copy_r(q, cc).start()
    for k in range(1, R):
        copy_l(k).start()
    for k in range(1, C):
        copy_x(k).start()

    lall[r] = lsend[...]
    xall[c] = x_ref[...]
    own = lax.div(r, Q) == c

    @pl.when(own)
    def _():
        rall[r] = rsend[lax.rem(r, Q)]

    qt = dot_nt(transposed(wq_ref[...]), xn).astype(BF16)
    gate = jax.nn.sigmoid(dot_nt(transposed(wg_ref[...]), xn))
    row_block = lax.broadcasted_iota(jnp.int32, (128, I), 0) // D
    for s in range(SL):
        gt[s] = gate[:, s * I : (s + 1) * I]
        for h in range(H):
            base = (h // group) * 128
            piece = qt[base : base + 128, s * I : (s + 1) * I].astype(F32)
            qbd[s * H + h] = jnp.where(row_block == h % group, piece, 0.0).astype(BF16)
    for k in range(PW):
        piece = wfin_ref[k * PW : (k + 1) * PW, :]
        for m in range(128 // PW):
            wd[k // 2, m * PW : (m + 1) * PW, (k % 2) * Z : (k % 2 + 1) * Z] = piece
    cf[...] = couple_ref[...].astype(F32).reshape(I * J, Z)
    woff = woff_ref[...].T
    w1 = woff.astype(BF16).astype(F32)
    w2 = (woff - w1).astype(BF16).astype(F32)
    w3 = (woff - w1 - w2).astype(BF16).astype(F32)
    woff_t = jnp.concatenate([w1, w2, w3, jnp.zeros_like(w1)], axis=0).astype(BF16)

    members = []
    for k in range(chains + 1):
        total = (label_ref[0] == k).astype(jnp.int32)
        for s in range(1, S):
            total = total + (label_ref[s] == k).astype(jnp.int32)
        members.append(total)

    for k in range(R):
        @pl.when(jnp.logical_not(jnp.logical_and(own, r == k)))
        def _(k=k):
            pltpu.make_async_remote_copy(
                src_ref=rsend.at[0], dst_ref=rall.at[k], send_sem=r_send.at[0],
                recv_sem=r_recv.at[k], device_id=(g, r, c), device_id_type=MESH,
            ).wait_recv()
    lane = lax.broadcasted_iota(jnp.int32, (16, 128), 1) // PW
    for k in range(R):
        tile = rall[k].astype(F32)
        for half in range(halves):
            for s in range(SL):
                rscr[pl.ds(half * 16 * S + k * SL + s, 16, stride=S), :] = jnp.where(
                    lane == half * SL + s, tile, 0.0
                )
    right = rscr[...].astype(BF16)

    def spread_right(cp, carry):
        res = dot_nn(right, wd[cp]).astype(BF16)
        for j in range(J):
            for e in range(2):
                bscr[
                    j // 2,
                    pl.ds(pl.multiple_of((2 * cp + e) * S, 16), S),
                    (j % 2) * Z : (j % 2 + 1) * Z,
                ] = res[j * S : (j + 1) * S, e * Z : (e + 1) * Z]
        return carry

    lax.fori_loop(0, PW // 2, spread_right, 0)

    for k in range(1, R):
        copy_l(k).wait_recv()
    for k in range(R):
        for s in range(SL):
            piece = lall[k, s].astype(F32)
            for b in range(I // 128):
                at = pl.ds(b * PW * S + k * SL + s, PW, stride=S)
                lscr[at, :] = piece[:, b * 128 : (b + 1) * 128]
    left = jnp.concatenate(
        [lscr[b * PW * S : (b + 1) * PW * S, :].T for b in range(I // 128)], axis=0
    ).astype(BF16)

    chain_z = chain_i[:, :Z]

    def pair_step(jj, carry):
        update = dot_nn(left, bscr[jj])
        normed = []
        for e in range(2):
            j = 2 * jj + e
            chain_j = chain_of(r * J + j, start_ref, chains)
            own_rows = members[0]
            for k in range(1, chains):
                own_rows = jnp.where(chain_j == k, members[k], own_rows)
            same = 1.0 / (jnp.full((1, Z), members[chains] + own_rows, jnp.int32).astype(F32) + 0.001)
            other = 1.0 / (jnp.full((1, Z), members[chains], jnp.int32).astype(F32) + 0.001)
            factor = jnp.where(chain_z == chain_j, same, other)
            at = pl.ds(j, I, stride=J)
            state = (cf[at, :] + update[:, e * Z : (e + 1) * Z] * factor).astype(BF16).astype(F32)
            cf[at, :] = state
            normed.append(standardize(state).astype(BF16))
        res = dot_nt(woff_t, jnp.concatenate(normed, axis=0))
        res = res[:H] + res[H : 2 * H] + res[2 * H : 3 * H]
        for e in range(2):
            for b in range(I // 128):
                at = pl.ds(b * H * J + 2 * jj + e, H, stride=J)
                biasf[at, :] = res[:, e * I + b * 128 : e * I + (b + 1) * 128]
        return carry

    lax.fori_loop(0, J // 2, pair_step, 0)

    for b in range(I // 128):
        ball[r, :, :, b * 128 : (b + 1) * 128] = (
            biasf[b * H * J : (b + 1) * H * J, :].astype(BF16).reshape(H, J, 128)
        )

    ZC = R // 2
    z, core = lax.div(r, 2), lax.rem(r, 2)
    sibling = 2 * z + 1 - core

    def copy_b(k):
        return pltpu.make_async_remote_copy(
            src_ref=ball.at[r], dst_ref=ball.at[r], send_sem=b_send.at[k], recv_sem=b_recv.at[k],
            device_id=(g, 2 * lax.rem(z + k, ZC) + core, c), device_id_type=MESH,
        )

    def copy_f(k):
        slot = 2 * lax.rem(z + ZC - k, ZC) + core
        return pltpu.make_async_remote_copy(
            src_ref=ball.at[slot], dst_ref=ball.at[slot], send_sem=f_send.at[k],
            recv_sem=f_recv.at[k], device_id=(g, sibling, c), device_id_type=MESH,
        )

    for k in range(1, ZC):
        copy_b(k).start()
    copy_f(0).start()

    pair_ref[...] = cf[...].astype(BF16).reshape(I, J, Z)

    for k in range(1, C):
        copy_x(k).wait_recv()
    wv_t = transposed(wkv_ref[:, inner:])
    for cc in range(C):
        block = standardize(xall[cc].astype(F32).reshape(SL * I, CH)).astype(BF16)
        keys = dot_nn(block, wkv_ref[:, :inner]).astype(BF16)
        vals = dot_nt(wv_t, block).astype(BF16)
        for s in range(SL):
            kscr[s, cc * I : (cc + 1) * I, :] = keys[s * I : (s + 1) * I]
            vt[s, :, cc * I : (cc + 1) * I] = vals[:, s * I : (s + 1) * I]
    chain_a = chain_of(lax.broadcasted_iota(jnp.int32, (A, I), 0), start_ref, chains)
    for s in range(SL):
        kept = jnp.logical_or(chain_a == labels[s], labels[s] == chains)
        madd[s] = jnp.where(kept, 0.0, -1000000000.0)

    for k in range(1, ZC):
        copy_b(k).wait_recv()
        copy_f(k).start()
    for k in range(ZC):
        copy_f(k).wait_recv()

    scale = 1.0 / math.sqrt(D)

    def attend(step, carry):
        s, h = lax.div(step, H), lax.rem(step, H)
        at = pl.ds(pl.multiple_of(lax.div(h, group) * 128, 128), 128)
        scores = dot_nn(kscr[s, :, at], qbd[step]) * scale
        scores = scores + ball[:, h].astype(F32).reshape(A, I) + madd[s]
        weights = jnp.exp(scores - jnp.max(scores, axis=0, keepdims=True))
        total = jnp.sum(weights, axis=0, keepdims=True)
        rows = pl.ds(pl.multiple_of(h * D, D), D)
        attended = dot_nn(vt[s, rows, :], weights.astype(BF16)) / total
        gated[s, rows, :] = (gt[s, rows, :] * attended).astype(BF16)
        return carry

    lax.fori_loop(0, SL * H, attend, 0)

    for s in range(SL):
        merged = dot_nn(transposed(gated[s]), wm_ref[...])
        out_ref[s] = (x_ref[s].astype(F32) + merged).astype(BF16)

    for q in range(Q):
        for cc in range(C):
            @pl.when(jnp.logical_not(jnp.logical_and(c * Q + q == r, cc == c)))
            def _(q=q, cc=cc):
                copy_r(q, cc).wait_send()
    for k in range(1, R):
        copy_l(k).wait_send()
    for k in range(1, C):
        copy_x(k).wait_send()
    for k in range(1, ZC):
        copy_b(k).wait_send()
    for k in range(ZC):
        copy_f(k).wait_send()


def per_device(R, C, homolog, couple, starts, labels, *weights):
    SL, I, CH = homolog.shape
    J, Z = couple.shape[1], couple.shape[2]
    S = labels.shape[0]
    wsrc, wtgt, wfin, woff, wq = weights[:5]
    PW, H, inner = wsrc.shape[1], woff.shape[1], wq.shape[1]
    A = C * I
    Q = I // J
    vmem = pl.BlockSpec(memory_space=pltpu.VMEM)
    smem = pl.BlockSpec(memory_space=pltpu.SMEM)
    dma = pltpu.SemaphoreType.DMA
    return pl.pallas_call(
        functools.partial(kernel, R, C),
        out_shape=(
            jax.ShapeDtypeStruct(homolog.shape, BF16),
            jax.ShapeDtypeStruct(couple.shape, BF16),
        ),
        in_specs=[smem, smem] + [vmem] * 10,
        out_specs=(vmem, vmem),
        scratch_shapes=[
            pltpu.VMEM((SL, PW, I), BF16),
            pltpu.VMEM((R, SL, PW, I), BF16),
            pltpu.VMEM((Q, 16, 128), BF16),
            pltpu.VMEM((R, 16, 128), BF16),
            pltpu.VMEM((C, SL, I, CH), BF16),
            pltpu.VMEM((I // 128 * PW * S, 128), F32),
            pltpu.VMEM((J * S, 128), F32),
            pltpu.VMEM((PW // 2, 128, 2 * Z), BF16),
            pltpu.VMEM((J // 2, PW * S, 2 * Z), BF16),
            pltpu.VMEM((I * J, Z), F32),
            pltpu.VMEM((I // 128 * H * J, 128), F32),
            pltpu.VMEM((R, H, J, I), BF16),
            pltpu.VMEM((SL * H, 128, I), BF16),
            pltpu.VMEM((SL, inner, I), F32),
            pltpu.VMEM((SL, A, inner), BF16),
            pltpu.VMEM((SL, inner, A), BF16),
            pltpu.VMEM((SL, A, I), F32),
            pltpu.VMEM((SL, inner, I), BF16),
            dma((R,)), dma((R,)), dma((R,)), dma((R,)), dma((C,)), dma((C,)),
            dma((R // 2,)), dma((R // 2,)), dma((R // 2,)), dma((R // 2,)),
        ],
        compiler_params=pltpu.CompilerParams(
            collective_id=0, has_side_effects=True, vmem_limit_bytes=56 * 2**20
        ),
    )(starts, labels, homolog, couple, *weights)


def solution(mesh):
    spec = (
        P(("groups", "row"), "col", None),
        P(("groups", "col"), "row", None),
    )
    return jax.shard_map(
        functools.partial(per_device, mesh.shape["row"], mesh.shape["col"]),
        mesh=mesh,
        in_specs=spec + (P("groups"), P("groups")) + (P(),) * 8,
        out_specs=spec,
        check_vma=False,
    )
```

```python
import functools
import math

import jax
import jax.numpy as jnp
from jax import lax
from jax.experimental import pallas as pl
from jax.experimental.pallas import tpu as pltpu
from jax.sharding import PartitionSpec as P

EPS = 1e-05
MESH = pl.DeviceIdType.MESH
F32 = jnp.float32
BF16 = jnp.bfloat16
UP, US, UA, UB = 4, 4, 4, 4


def standardize(values):
    center = values - jnp.mean(values, axis=-1, keepdims=True)
    spread = jnp.mean(center * center, axis=-1, keepdims=True)
    return center * lax.rsqrt(spread + EPS)


def dot_nt(a, b):
    return lax.dot_general(a, b, (((1,), (1,)), ((), ())), preferred_element_type=F32)


def dot_nn(a, b):
    return jnp.dot(a, b, preferred_element_type=F32)


def transposed(a):
    return a.astype(F32).T.astype(BF16)


def chain_of(position, start_ref, chains):
    chain = (position >= start_ref[0]).astype(jnp.int32)
    for k in range(1, chains):
        chain = chain + (position >= start_ref[k]).astype(jnp.int32)
    return chain - 1


def kernel(
    R, C,
    start_ref, label_ref, x_ref, couple_ref, wsrc_ref, wtgt_ref, wfin_ref, woff_ref,
    wq_ref, wkv_ref, wg_ref, wm_ref,
    out_ref, pair_ref,
    lsend, lall, rsend, rall, xall, lscr, rscr, wd, bscr, cf, biasf, ball,
    qbd, gt, kscr, vt, madd, gated, held,
    l_send, l_recv, r_send, r_recv, x_send, x_recv, b_send, b_recv, f_send, f_recv,
):
    SL, I, CH = x_ref.shape
    J, Z = couple_ref.shape[1], couple_ref.shape[2]
    S = label_ref.shape[0]
    chains = start_ref.shape[0]
    H = woff_ref.shape[0]
    PW = wsrc_ref.shape[0]
    inner = wq_ref.shape[1]
    D = inner // H
    A = C * I
    Q = I // J
    group = 128 // D
    halves = J // 16
    g = lax.axis_index("groups")
    r = lax.axis_index("row")
    c = lax.axis_index("col")
    n = R * C
    me = r * C + c

    barrier = pltpu.get_barrier_semaphore()

    def greet(k, carry):
        t = lax.rem(me + k, n)
        pl.semaphore_signal(
            barrier, inc=1, device_id=(g, lax.div(t, C), lax.rem(t, C)), device_id_type=MESH
        )
        return carry

    lax.fori_loop(1, n, greet, 0)

    xn = standardize(x_ref[...].astype(F32).reshape(SL * I, CH))
    chain_i = chain_of(
        c * I + lax.broadcasted_iota(jnp.int32, (I, CH), 0), start_ref, chains
    )
    labels = [label_ref[r * SL + s] for s in range(SL)]
    xm = []
    for s in range(SL):
        kept = jnp.logical_or(chain_i == labels[s], labels[s] == chains)
        xm.append(jnp.where(kept, xn[s * I : (s + 1) * I], 0.0).astype(BF16))
    xn = xn.astype(BF16)
    wsrc_t = wsrc_ref[...]
    for s in range(SL):
        lsend[s] = dot_nt(wsrc_t, xm[s]).astype(BF16)
    wt = wtgt_ref[...].astype(F32)
    wt = jnp.concatenate([wt] * (128 // PW), axis=0)
    wt_row = lax.broadcasted_iota(jnp.int32, wt.shape, 0) // PW
    packed = None
    for half in range(halves):
        for s in range(SL):
            k = half * SL + s
            rows = xm[s].reshape(Q, halves, 16, CH)[:, half].reshape(Q * 16, CH)
            part = dot_nt(rows, jnp.where(wt_row == k, wt, 0.0).astype(BF16))
            packed = part if packed is None else packed + part
    rsend[...] = packed.astype(BF16).reshape(Q, 16, 128)

    pl.semaphore_wait(barrier, n - 1)

    def copy_l(k):
        t = lax.rem(r + k, R)
        return pltpu.make_async_remote_copy(
            src_ref=lsend, dst_ref=lall.at[r], send_sem=l_send.at[k], recv_sem=l_recv.at[k],
            device_id=(g, t, c), device_id_type=MESH,
        )

    def copy_r(q, cc):
        return pltpu.make_async_remote_copy(
            src_ref=rsend.at[q], dst_ref=rall.at[r], send_sem=r_send.at[q * C + cc],
            recv_sem=r_recv.at[r], device_id=(g, c * Q + q, cc), device_id_type=MESH,
        )

    def copy_x(k):
        return pltpu.make_async_remote_copy(
            src_ref=x_ref, dst_ref=xall.at[c], send_sem=x_send.at[k], recv_sem=x_recv.at[k],
            device_id=(g, r, lax.rem(c + k, C)), device_id_type=MESH,
        )

    for q in range(Q):
        for cc in range(C):
            @pl.when(jnp.logical_not(jnp.logical_and(c * Q + q == r, cc == c)))
            def _(q=q, cc=cc):
                copy_r(q, cc).start()
    for k in range(1, R):
        copy_l(k).start()
    for k in range(1, C):
        copy_x(k).start()

    lall[r] = lsend[...]
    xall[c] = x_ref[...]
    own = lax.div(r, Q) == c

    @pl.when(own)
    def _():
        rall[r] = rsend[lax.rem(r, Q)]

    qt = dot_nt(transposed(wq_ref[...]), xn).astype(BF16)
    gate = jax.nn.sigmoid(dot_nt(transposed(wg_ref[...]), xn))
    row_block = lax.broadcasted_iota(jnp.int32, (128, I), 0) // D
    for s in range(SL):
        gt[s] = gate[:, s * I : (s + 1) * I]
        for h in range(H):
            base = (h // group) * 128
            piece = qt[base : base + 128, s * I : (s + 1) * I].astype(F32)
            qbd[s * H + h] = jnp.where(row_block == h % group, piece, 0.0).astype(BF16)
    for k in range(PW):
        piece = wfin_ref[k * PW : (k + 1) * PW, :]
        for m in range(128 // PW):
            wd[k // 2, m * PW : (m + 1) * PW, (k % 2) * Z : (k % 2 + 1) * Z] = piece
    cf[...] = couple_ref[...].astype(F32).reshape(I * J, Z)
    woff = woff_ref[...]
    w1 = woff.astype(BF16).astype(F32)
    w2 = (woff - w1).astype(BF16).astype(F32)
    w3 = (woff - w1 - w2).astype(BF16).astype(F32)
    woff_t = jnp.concatenate([w1, w2, w3, jnp.zeros_like(w1)], axis=0).astype(BF16)

    members = []
    for k in range(chains + 1):
        total = (label_ref[0] == k).astype(jnp.int32)
        for s in range(1, S):
            total = total + (label_ref[s] == k).astype(jnp.int32)
        members.append(total)

    for k in range(R):
        @pl.when(jnp.logical_not(jnp.logical_and(own, r == k)))
        def _(k=k):
            pltpu.make_async_remote_copy(
                src_ref=rsend.at[0], dst_ref=rall.at[k], send_sem=r_send.at[0],
                recv_sem=r_recv.at[k], device_id=(g, r, c), device_id_type=MESH,
            ).wait_recv()
    lane = lax.broadcasted_iota(jnp.int32, (16, 128), 1) // PW
    for k in range(R):
        tile = rall[k].astype(F32)
        for half in range(halves):
            for s in range(SL):
                rscr[pl.ds(half * 16 * S + k * SL + s, 16, stride=S), :] = jnp.where(
                    lane == half * SL + s, tile, 0.0
                )
    right = rscr[...].astype(BF16)

    def spread_right(cp, carry):
        res = dot_nn(right, wd[cp]).astype(BF16)
        for j in range(J):
            for e in range(2):
                bscr[
                    j // 2,
                    pl.ds(pl.multiple_of((2 * cp + e) * S, 16), S),
                    (j % 2) * Z : (j % 2 + 1) * Z,
                ] = res[j * S : (j + 1) * S, e * Z : (e + 1) * Z]
        return carry

    lax.fori_loop(0, PW // 2, spread_right, 0, unroll=UB)

    for k in range(1, R):
        copy_l(k).wait_recv()
    for k in range(R):
        for s in range(SL):
            piece = lall[k, s].astype(F32)
            for b in range(I // 128):
                at = pl.ds(b * PW * S + k * SL + s, PW, stride=S)
                lscr[at, :] = piece[:, b * 128 : (b + 1) * 128]
    left = jnp.concatenate(
        [lscr[b * PW * S : (b + 1) * PW * S, :].T for b in range(I // 128)], axis=0
    ).astype(BF16)

    chain_z = chain_i[:, :Z]

    def pair_step(jj, carry):
        update = dot_nn(left, bscr[jj])
        normed = []
        for e in range(2):
            j = 2 * jj + e
            chain_j = chain_of(r * J + j, start_ref, chains)
            own_rows = members[0]
            for k in range(1, chains):
                own_rows = jnp.where(chain_j == k, members[k], own_rows)
            same = 1.0 / (jnp.full((1, Z), members[chains] + own_rows, jnp.int32).astype(F32) + 0.001)
            other = 1.0 / (jnp.full((1, Z), members[chains], jnp.int32).astype(F32) + 0.001)
            factor = jnp.where(chain_z == chain_j, same, other)
            at = pl.ds(j, I, stride=J)
            state = (cf[at, :] + update[:, e * Z : (e + 1) * Z] * factor).astype(BF16).astype(F32)
            cf[at, :] = state
            normed.append(standardize(state).astype(BF16))
        res = dot_nt(woff_t, jnp.concatenate(normed, axis=0))
        res = res[:H] + res[H : 2 * H] + res[2 * H : 3 * H]
        for e in range(2):
            for b in range(I // 128):
                at = pl.ds(b * H * 16 + lax.rem(2 * jj, 16) + e, H, stride=16)
                biasf[at, :] = res[:, e * I + b * 128 : e * I + (b + 1) * 128]
        return carry

    ZC = R // 2
    z, core = lax.div(r, 2), lax.rem(r, 2)
    sibling = 2 * z + 1 - core

    def copy_b(half, k):
        return pltpu.make_async_remote_copy(
            src_ref=ball.at[r, half], dst_ref=ball.at[r, half],
            send_sem=b_send.at[half, k], recv_sem=b_recv.at[half, k],
            device_id=(g, 2 * lax.rem(z + k, ZC) + core, c), device_id_type=MESH,
        )

    def copy_f(half, k):
        slot = 2 * lax.rem(z + ZC - k, ZC) + core
        return pltpu.make_async_remote_copy(
            src_ref=ball.at[slot, half], dst_ref=ball.at[slot, half],
            send_sem=f_send.at[half, k], recv_sem=f_recv.at[half, k],
            device_id=(g, sibling, c), device_id_type=MESH,
        )

    for half in range(halves):
        lax.fori_loop(half * 8, half * 8 + 8, pair_step, 0, unroll=UP)
        for b in range(I // 128):
            ball[r, half, :, :, b * 128 : (b + 1) * 128] = (
                biasf[b * H * 16 : (b + 1) * H * 16, :].astype(BF16).reshape(H, 16, 128)
            )
        for k in range(1, ZC):
            copy_b(half, k).start()
        copy_f(half, 0).start()

    pair_ref[...] = cf[...].astype(BF16).reshape(I, J, Z)

    for k in range(1, C):
        copy_x(k).wait_recv()
    wv_t = transposed(wkv_ref[:, inner:])
    for cc in range(C):
        block = standardize(xall[cc].astype(F32).reshape(SL * I, CH)).astype(BF16)
        keys = dot_nn(block, wkv_ref[:, :inner]).astype(BF16)
        vals = dot_nt(wv_t, block).astype(BF16)
        for s in range(SL):
            kscr[s, cc * I : (cc + 1) * I, :] = keys[s * I : (s + 1) * I]
            vt[s, :, cc * I : (cc + 1) * I] = vals[:, s * I : (s + 1) * I]
    chain_a = chain_of(lax.broadcasted_iota(jnp.int32, (A, I), 0), start_ref, chains)
    for s in range(SL):
        kept = jnp.logical_or(chain_a == labels[s], labels[s] == chains)
        madd[s] = jnp.where(kept, 0.0, -1000000000.0)

    scale = 1.0 / math.sqrt(D)

    def score(step, carry):
        s, h = lax.div(step, H), lax.rem(step, H)
        at = pl.ds(pl.multiple_of(lax.div(h, group) * 128, 128), 128)
        held[step] = dot_nn(kscr[s, :, at], qbd[step]) * scale + madd[s]
        return carry

    def forward(half):
        for k in range(1, ZC):
            copy_b(half, k).wait_recv()
            copy_f(half, k).start()

    for half in range(halves - 1):
        forward(half)
    lax.fori_loop(0, SL * H, score, 0, unroll=US)
    forward(halves - 1)
    for half in range(halves):
        for k in range(ZC):
            copy_f(half, k).wait_recv()

    def attend(step, carry):
        s, h = lax.div(step, H), lax.rem(step, H)
        scores = held[step] + ball[:, :, h].astype(F32).reshape(A, I)
        weights = jnp.exp(scores - jnp.max(scores, axis=0, keepdims=True))
        total = jnp.sum(weights, axis=0, keepdims=True)
        rows = pl.ds(pl.multiple_of(h * D, D), D)
        attended = dot_nn(vt[s, rows, :], weights.astype(BF16)) / total
        gated[s, rows, :] = (gt[s, rows, :] * attended).astype(BF16)
        return carry

    lax.fori_loop(0, SL * H, attend, 0, unroll=UA)

    for s in range(SL):
        merged = dot_nn(transposed(gated[s]), wm_ref[...])
        out_ref[s] = (x_ref[s].astype(F32) + merged).astype(BF16)

    for q in range(Q):
        for cc in range(C):
            @pl.when(jnp.logical_not(jnp.logical_and(c * Q + q == r, cc == c)))
            def _(q=q, cc=cc):
                copy_r(q, cc).wait_send()
    for k in range(1, R):
        copy_l(k).wait_send()
    for k in range(1, C):
        copy_x(k).wait_send()
    for half in range(halves):
        for k in range(1, ZC):
            copy_b(half, k).wait_send()
        for k in range(ZC):
            copy_f(half, k).wait_send()


def per_device(R, C, homolog, couple, starts, labels, *weights):
    SL, I, CH = homolog.shape
    J, Z = couple.shape[1], couple.shape[2]
    S = labels.shape[0]
    wsrc, wtgt, wfin, woff, wq = weights[:5]
    PW, H, inner = wsrc.shape[1], woff.shape[1], wq.shape[1]
    A = C * I
    Q = I // J
    vmem = pl.BlockSpec(memory_space=pltpu.VMEM)
    smem = pl.BlockSpec(memory_space=pltpu.SMEM)
    dma = pltpu.SemaphoreType.DMA
    return pl.pallas_call(
        functools.partial(kernel, R, C),
        out_shape=(
            jax.ShapeDtypeStruct(homolog.shape, BF16),
            jax.ShapeDtypeStruct(couple.shape, BF16),
        ),
        in_specs=[smem, smem] + [vmem] * 10,
        out_specs=(vmem, vmem),
        scratch_shapes=[
            pltpu.VMEM((SL, PW, I), BF16),
            pltpu.VMEM((R, SL, PW, I), BF16),
            pltpu.VMEM((Q, 16, 128), BF16),
            pltpu.VMEM((R, 16, 128), BF16),
            pltpu.VMEM((C, SL, I, CH), BF16),
            pltpu.VMEM((I // 128 * PW * S, 128), F32),
            pltpu.VMEM((J * S, 128), F32),
            pltpu.VMEM((PW // 2, 128, 2 * Z), BF16),
            pltpu.VMEM((J // 2, PW * S, 2 * Z), BF16),
            pltpu.VMEM((I * J, Z), F32),
            pltpu.VMEM((I // 128 * H * 16, 128), F32),
            pltpu.VMEM((R, J // 16, H, 16, I), BF16),
            pltpu.VMEM((SL * H, 128, I), BF16),
            pltpu.VMEM((SL, inner, I), F32),
            pltpu.VMEM((SL, A, inner), BF16),
            pltpu.VMEM((SL, inner, A), BF16),
            pltpu.VMEM((SL, A, I), F32),
            pltpu.VMEM((SL, inner, I), BF16),
            pltpu.VMEM((SL * H, A, I), F32),
            dma((R,)), dma((R,)), dma((R,)), dma((R,)), dma((C,)), dma((C,)),
            *[dma((J // 16, R // 2))] * 4,
        ],
        compiler_params=pltpu.CompilerParams(
            collective_id=0, has_side_effects=True, vmem_limit_bytes=61 * 2**20
        ),
    )(starts, labels, homolog, couple, wsrc.T, wtgt.T, wfin, woff.T, *weights[4:])


def solution(mesh):
    spec = (
        P(("groups", "row"), "col", None),
        P(("groups", "col"), "row", None),
    )
    return jax.shard_map(
        functools.partial(per_device, mesh.shape["row"], mesh.shape["col"]),
        mesh=mesh,
        in_specs=spec + (P("groups"), P("groups")) + (P(),) * 8,
        out_specs=spec,
        check_vma=False,
    )
```

```python
import functools
import math

import jax
import jax.numpy as jnp
from jax import lax
from jax.experimental import pallas as pl
from jax.experimental.pallas import tpu as pltpu
from jax.sharding import PartitionSpec as P

EPS = 1e-05
MESH = pl.DeviceIdType.MESH
F32 = jnp.float32
BF16 = jnp.bfloat16
UP, US, UA, UB = 8, 4, 8, 8


def standardize(values):
    center = values - jnp.mean(values, axis=-1, keepdims=True)
    spread = jnp.mean(center * center, axis=-1, keepdims=True)
    return center * lax.rsqrt(spread + EPS)


def dot_nt(a, b):
    return lax.dot_general(a, b, (((1,), (1,)), ((), ())), preferred_element_type=F32)


def dot_nn(a, b):
    return jnp.dot(a, b, preferred_element_type=F32)


def transposed(a):
    return a.astype(F32).T.astype(BF16)


def chain_of(position, start_ref, chains):
    chain = (position >= start_ref[0]).astype(jnp.int32)
    for k in range(1, chains):
        chain = chain + (position >= start_ref[k]).astype(jnp.int32)
    return chain - 1


def kernel(
    R, C,
    start_ref, label_ref, x_ref, couple_ref, wsrc_ref, wtgt_ref, wfin_ref, woff_ref,
    wq_ref, wkv_ref, wg_ref, wm_ref,
    out_ref, pair_ref,
    lsend, lall, rsend, rall, xall, lscr, rscr, wd, bscr, cf, biasf, ball,
    qbd, gt, kscr, vt, madd, gated, held,
    l_send, l_recv, r_send, r_recv, x_send, x_recv, b_send, b_recv, f_send, f_recv,
):
    SL, I, CH = x_ref.shape
    J, Z = couple_ref.shape[1], couple_ref.shape[2]
    S = label_ref.shape[0]
    chains = start_ref.shape[0]
    H = woff_ref.shape[0]
    PW = wsrc_ref.shape[0]
    inner = wq_ref.shape[1]
    D = inner // H
    A = C * I
    Q = I // J
    group = 128 // D
    halves = J // 16
    g = lax.axis_index("groups")
    r = lax.axis_index("row")
    c = lax.axis_index("col")
    n = R * C
    me = r * C + c

    barrier = pltpu.get_barrier_semaphore()

    def greet(k, carry):
        t = lax.rem(me + k, n)
        pl.semaphore_signal(
            barrier, inc=1, device_id=(g, lax.div(t, C), lax.rem(t, C)), device_id_type=MESH
        )
        return carry

    lax.fori_loop(1, n, greet, 0)

    xn = standardize(x_ref[...].astype(F32).reshape(SL * I, CH))
    chain_i = chain_of(
        c * I + lax.broadcasted_iota(jnp.int32, (I, CH), 0), start_ref, chains
    )
    labels = [label_ref[r * SL + s] for s in range(SL)]
    xm = []
    for s in range(SL):
        kept = jnp.logical_or(chain_i == labels[s], labels[s] == chains)
        xm.append(jnp.where(kept, xn[s * I : (s + 1) * I], 0.0).astype(BF16))
    xn = xn.astype(BF16)
    wsrc_t = wsrc_ref[...]
    for s in range(SL):
        lsend[s] = dot_nt(wsrc_t, xm[s]).astype(BF16)
    wt = wtgt_ref[...].astype(F32)
    wt = jnp.concatenate([wt] * (128 // PW), axis=0)
    wt_row = lax.broadcasted_iota(jnp.int32, wt.shape, 0) // PW
    packed = None
    for half in range(halves):
        for s in range(SL):
            k = half * SL + s
            rows = xm[s].reshape(Q, halves, 16, CH)[:, half].reshape(Q * 16, CH)
            part = dot_nt(rows, jnp.where(wt_row == k, wt, 0.0).astype(BF16))
            packed = part if packed is None else packed + part
    rsend[...] = packed.astype(BF16).reshape(Q, 16, 128)

    pl.semaphore_wait(barrier, n - 1)

    def copy_l(k):
        t = lax.rem(r + k, R)
        return pltpu.make_async_remote_copy(
            src_ref=lsend, dst_ref=lall.at[r], send_sem=l_send.at[k], recv_sem=l_recv.at[k],
            device_id=(g, t, c), device_id_type=MESH,
        )

    def copy_r(q, cc):
        return pltpu.make_async_remote_copy(
            src_ref=rsend.at[q], dst_ref=rall.at[r], send_sem=r_send.at[q * C + cc],
            recv_sem=r_recv.at[r], device_id=(g, c * Q + q, cc), device_id_type=MESH,
        )

    def copy_x(k):
        return pltpu.make_async_remote_copy(
            src_ref=x_ref, dst_ref=xall.at[c], send_sem=x_send.at[k], recv_sem=x_recv.at[k],
            device_id=(g, r, lax.rem(c + k, C)), device_id_type=MESH,
        )

    for q in range(Q):
        for cc in range(C):
            @pl.when(jnp.logical_not(jnp.logical_and(c * Q + q == r, cc == c)))
            def _(q=q, cc=cc):
                copy_r(q, cc).start()
    for k in range(1, R):
        copy_l(k).start()
    for k in range(1, C):
        copy_x(k).start()

    lall[r] = lsend[...]
    xall[c] = x_ref[...]
    own = lax.div(r, Q) == c

    @pl.when(own)
    def _():
        rall[r] = rsend[lax.rem(r, Q)]

    qt = dot_nt(transposed(wq_ref[...]), xn).astype(BF16)
    gate = jax.nn.sigmoid(dot_nt(transposed(wg_ref[...]), xn))
    row_block = lax.broadcasted_iota(jnp.int32, (128, I), 0) // D
    for s in range(SL):
        gt[s] = gate[:, s * I : (s + 1) * I]
        for h in range(H):
            base = (h // group) * 128
            piece = qt[base : base + 128, s * I : (s + 1) * I].astype(F32)
            qbd[s * H + h] = jnp.where(row_block == h % group, piece, 0.0).astype(BF16)
    for k in range(PW):
        piece = wfin_ref[k * PW : (k + 1) * PW, :]
        for m in range(128 // PW):
            wd[k // 2, m * PW : (m + 1) * PW, (k % 2) * Z : (k % 2 + 1) * Z] = piece
    cf[...] = couple_ref[...].astype(F32).reshape(I * J, Z)
    woff = woff_ref[...]
    w1 = woff.astype(BF16).astype(F32)
    w2 = (woff - w1).astype(BF16).astype(F32)
    w3 = (woff - w1 - w2).astype(BF16).astype(F32)
    woff_t = jnp.concatenate([w1, w2, w3, jnp.zeros_like(w1)], axis=0).astype(BF16)

    members = []
    for k in range(chains + 1):
        total = (label_ref[0] == k).astype(jnp.int32)
        for s in range(1, S):
            total = total + (label_ref[s] == k).astype(jnp.int32)
        members.append(total)

    for k in range(R):
        @pl.when(jnp.logical_not(jnp.logical_and(own, r == k)))
        def _(k=k):
            pltpu.make_async_remote_copy(
                src_ref=rsend.at[0], dst_ref=rall.at[k], send_sem=r_send.at[0],
                recv_sem=r_recv.at[k], device_id=(g, r, c), device_id_type=MESH,
            ).wait_recv()
    lane = lax.broadcasted_iota(jnp.int32, (16, 128), 1) // PW
    for k in range(R):
        tile = rall[k].astype(F32)
        for half in range(halves):
            for s in range(SL):
                rscr[pl.ds(half * 16 * S + k * SL + s, 16, stride=S), :] = jnp.where(
                    lane == half * SL + s, tile, 0.0
                )
    right = rscr[...].astype(BF16)

    def spread_right(cp, carry):
        res = dot_nn(right, wd[cp]).astype(BF16)
        for j in range(J):
            for e in range(2):
                bscr[
                    j // 2,
                    pl.ds(pl.multiple_of((2 * cp + e) * S, 16), S),
                    (j % 2) * Z : (j % 2 + 1) * Z,
                ] = res[j * S : (j + 1) * S, e * Z : (e + 1) * Z]
        return carry

    lax.fori_loop(0, PW // 2, spread_right, 0, unroll=UB)

    for k in range(1, R):
        copy_l(k).wait_recv()
    for k in range(R):
        for s in range(SL):
            piece = lall[k, s].astype(F32)
            for b in range(I // 128):
                at = pl.ds(b * PW * S + k * SL + s, PW, stride=S)
                lscr[at, :] = piece[:, b * 128 : (b + 1) * 128]
    left = jnp.concatenate(
        [lscr[b * PW * S : (b + 1) * PW * S, :].T for b in range(I // 128)], axis=0
    ).astype(BF16)

    chain_z = chain_i[:, :Z]

    def pair_step(jj, carry):
        update = dot_nn(left, bscr[jj])
        normed = []
        for e in range(2):
            j = 2 * jj + e
            chain_j = chain_of(r * J + j, start_ref, chains)
            own_rows = members[0]
            for k in range(1, chains):
                own_rows = jnp.where(chain_j == k, members[k], own_rows)
            same = 1.0 / (jnp.full((1, Z), members[chains] + own_rows, jnp.int32).astype(F32) + 0.001)
            other = 1.0 / (jnp.full((1, Z), members[chains], jnp.int32).astype(F32) + 0.001)
            factor = jnp.where(chain_z == chain_j, same, other)
            at = pl.ds(j, I, stride=J)
            state = (cf[at, :] + update[:, e * Z : (e + 1) * Z] * factor).astype(BF16).astype(F32)
            cf[at, :] = state
            normed.append(standardize(state).astype(BF16))
        res = dot_nt(woff_t, jnp.concatenate(normed, axis=0))
        res = res[:H] + res[H : 2 * H] + res[2 * H : 3 * H]
        for e in range(2):
            for b in range(I // 128):
                at = pl.ds(b * H * 16 + lax.rem(2 * jj, 16) + e, H, stride=16)
                biasf[at, :] = res[:, e * I + b * 128 : e * I + (b + 1) * 128]
        return carry

    ZC = R // 2
    z, core = lax.div(r, 2), lax.rem(r, 2)
    sibling = 2 * z + 1 - core

    def copy_b(half, k):
        return pltpu.make_async_remote_copy(
            src_ref=ball.at[r, half], dst_ref=ball.at[r, half],
            send_sem=b_send.at[half, k], recv_sem=b_recv.at[half, k],
            device_id=(g, 2 * lax.rem(z + k, ZC) + core, c), device_id_type=MESH,
        )

    def copy_f(half, k):
        slot = 2 * lax.rem(z + ZC - k, ZC) + core
        return pltpu.make_async_remote_copy(
            src_ref=ball.at[slot, half], dst_ref=ball.at[slot, half],
            send_sem=f_send.at[half, k], recv_sem=f_recv.at[half, k],
            device_id=(g, sibling, c), device_id_type=MESH,
        )

    for half in range(halves):
        lax.fori_loop(half * 8, half * 8 + 8, pair_step, 0, unroll=UP)
        for b in range(I // 128):
            ball[r, half, :, :, b * 128 : (b + 1) * 128] = (
                biasf[b * H * 16 : (b + 1) * H * 16, :].astype(BF16).reshape(H, 16, 128)
            )
        for k in range(1, ZC):
            copy_b(half, k).start()
        copy_f(half, 0).start()

    pair_ref[...] = cf[...].astype(BF16).reshape(I, J, Z)

    for k in range(1, C):
        copy_x(k).wait_recv()
    wv_t = transposed(wkv_ref[:, inner:])
    for cc in range(C):
        block = standardize(xall[cc].astype(F32).reshape(SL * I, CH)).astype(BF16)
        keys = dot_nn(block, wkv_ref[:, :inner]).astype(BF16)
        vals = dot_nt(wv_t, block).astype(BF16)
        for s in range(SL):
            kscr[s, cc * I : (cc + 1) * I, :] = keys[s * I : (s + 1) * I]
            vt[s, :, cc * I : (cc + 1) * I] = vals[:, s * I : (s + 1) * I]
    chain_a = chain_of(lax.broadcasted_iota(jnp.int32, (A, I), 0), start_ref, chains)
    for s in range(SL):
        kept = jnp.logical_or(chain_a == labels[s], labels[s] == chains)
        madd[s] = jnp.where(kept, 0.0, -1000000000.0)

    scale = 1.0 / math.sqrt(D)

    def score(step, carry):
        s, h = lax.div(step, H), lax.rem(step, H)
        at = pl.ds(pl.multiple_of(lax.div(h, group) * 128, 128), 128)
        held[step] = dot_nn(kscr[s, :, at], qbd[step]) * scale + madd[s]
        return carry

    def forward(half):
        for k in range(1, ZC):
            copy_b(half, k).wait_recv()
            copy_f(half, k).start()

    for half in range(halves - 1):
        forward(half)
    lax.fori_loop(0, SL * H, score, 0, unroll=US)
    forward(halves - 1)
    for half in range(halves):
        for k in range(ZC):
            copy_f(half, k).wait_recv()

    def attend(step, carry):
        s, h = lax.div(step, H), lax.rem(step, H)
        scores = held[step] + ball[:, :, h].astype(F32).reshape(A, I)
        weights = jnp.exp(scores - jnp.max(scores, axis=0, keepdims=True))
        total = jnp.sum(weights, axis=0, keepdims=True)
        rows = pl.ds(pl.multiple_of(h * D, D), D)
        attended = dot_nn(vt[s, rows, :], weights.astype(BF16)) / total
        gated[s, rows, :] = (gt[s, rows, :] * attended).astype(BF16)
        return carry

    lax.fori_loop(0, SL * H, attend, 0, unroll=UA)

    for s in range(SL):
        merged = dot_nn(transposed(gated[s]), wm_ref[...])
        out_ref[s] = (x_ref[s].astype(F32) + merged).astype(BF16)

    for q in range(Q):
        for cc in range(C):
            @pl.when(jnp.logical_not(jnp.logical_and(c * Q + q == r, cc == c)))
            def _(q=q, cc=cc):
                copy_r(q, cc).wait_send()
    for k in range(1, R):
        copy_l(k).wait_send()
    for k in range(1, C):
        copy_x(k).wait_send()
    for half in range(halves):
        for k in range(1, ZC):
            copy_b(half, k).wait_send()
        for k in range(ZC):
            copy_f(half, k).wait_send()


def per_device(R, C, homolog, couple, starts, labels, *weights):
    SL, I, CH = homolog.shape
    J, Z = couple.shape[1], couple.shape[2]
    S = labels.shape[0]
    wsrc, wtgt, wfin, woff, wq = weights[:5]
    PW, H, inner = wsrc.shape[1], woff.shape[1], wq.shape[1]
    A = C * I
    Q = I // J
    vmem = pl.BlockSpec(memory_space=pltpu.VMEM)
    smem = pl.BlockSpec(memory_space=pltpu.SMEM)
    dma = pltpu.SemaphoreType.DMA
    return pl.pallas_call(
        functools.partial(kernel, R, C),
        out_shape=(
            jax.ShapeDtypeStruct(homolog.shape, BF16),
            jax.ShapeDtypeStruct(couple.shape, BF16),
        ),
        in_specs=[smem, smem] + [vmem] * 10,
        out_specs=(vmem, vmem),
        scratch_shapes=[
            pltpu.VMEM((SL, PW, I), BF16),
            pltpu.VMEM((R, SL, PW, I), BF16),
            pltpu.VMEM((Q, 16, 128), BF16),
            pltpu.VMEM((R, 16, 128), BF16),
            pltpu.VMEM((C, SL, I, CH), BF16),
            pltpu.VMEM((I // 128 * PW * S, 128), F32),
            pltpu.VMEM((J * S, 128), F32),
            pltpu.VMEM((PW // 2, 128, 2 * Z), BF16),
            pltpu.VMEM((J // 2, PW * S, 2 * Z), BF16),
            pltpu.VMEM((I * J, Z), F32),
            pltpu.VMEM((I // 128 * H * 16, 128), F32),
            pltpu.VMEM((R, J // 16, H, 16, I), BF16),
            pltpu.VMEM((SL * H, 128, I), BF16),
            pltpu.VMEM((SL, inner, I), F32),
            pltpu.VMEM((SL, A, inner), BF16),
            pltpu.VMEM((SL, inner, A), BF16),
            pltpu.VMEM((SL, A, I), F32),
            pltpu.VMEM((SL, inner, I), BF16),
            pltpu.VMEM((SL * H, A, I), F32),
            dma((R,)), dma((R,)), dma((R,)), dma((R,)), dma((C,)), dma((C,)),
            *[dma((J // 16, R // 2))] * 4,
        ],
        compiler_params=pltpu.CompilerParams(
            collective_id=0, has_side_effects=True, vmem_limit_bytes=61 * 2**20
        ),
    )(starts, labels, homolog, couple, wsrc.T, wtgt.T, wfin, woff.T, *weights[4:])


def solution(mesh):
    spec = (
        P(("groups", "row"), "col", None),
        P(("groups", "col"), "row", None),
    )
    return jax.shard_map(
        functools.partial(per_device, mesh.shape["row"], mesh.shape["col"]),
        mesh=mesh,
        in_specs=spec + (P("groups"), P("groups")) + (P(),) * 8,
        out_specs=spec,
        check_vma=False,
    )
```

```python
import functools
import math

import jax
import jax.numpy as jnp
from jax import lax
from jax.experimental import pallas as pl
from jax.experimental.pallas import tpu as pltpu
from jax.sharding import PartitionSpec as P

EPS = 1e-05
MESH = pl.DeviceIdType.MESH
F32 = jnp.float32
BF16 = jnp.bfloat16
UP, US, UA, UB = 8, 4, 8, 8


def standardize(values):
    center = values - jnp.mean(values, axis=-1, keepdims=True)
    spread = jnp.mean(center * center, axis=-1, keepdims=True)
    return center * lax.rsqrt(spread + EPS)


def dot_nt(a, b):
    return lax.dot_general(a, b, (((1,), (1,)), ((), ())), preferred_element_type=F32)


def dot_nn(a, b):
    return jnp.dot(a, b, preferred_element_type=F32)


def transposed(a):
    return a.astype(F32).T.astype(BF16)


def chain_of(position, start_ref, chains):
    chain = (position >= start_ref[0]).astype(jnp.int32)
    for k in range(1, chains):
        chain = chain + (position >= start_ref[k]).astype(jnp.int32)
    return chain - 1


def kernel(
    R, C,
    start_ref, label_ref, x_ref, couple_ref, wsrc_ref, wtgt_ref, wfin_ref, woff_ref,
    wq_ref, wkv_ref, wg_ref, wm_ref,
    out_ref, pair_ref,
    lsend, lall, rsend, rall, xall, lscr, rscr, wd, bscr, cf, biasf, ball,
    qbd, gt, kscr, vt, madd, gated, held,
    l_send, l_recv, r_send, r_recv, x_send, x_recv, b_send, b_recv, f_send, f_recv,
):
    SL, I, CH = x_ref.shape
    J, Z = couple_ref.shape[1], couple_ref.shape[2]
    S = label_ref.shape[0]
    chains = start_ref.shape[0]
    H = woff_ref.shape[0]
    PW = wsrc_ref.shape[0]
    inner = wq_ref.shape[1]
    D = inner // H
    A = C * I
    Q = I // J
    group = 128 // D
    halves = J // 16
    g = lax.axis_index("groups")
    r = lax.axis_index("row")
    c = lax.axis_index("col")
    n = R * C
    me = r * C + c

    barrier = pltpu.get_barrier_semaphore()

    def greet(k, carry):
        t = lax.rem(me + k, n)
        pl.semaphore_signal(
            barrier, inc=1, device_id=(g, lax.div(t, C), lax.rem(t, C)), device_id_type=MESH
        )
        return carry

    lax.fori_loop(1, n, greet, 0)

    xn = standardize(x_ref[...].astype(F32).reshape(SL * I, CH))
    chain_i = chain_of(
        c * I + lax.broadcasted_iota(jnp.int32, (I, CH), 0), start_ref, chains
    )
    labels = [label_ref[r * SL + s] for s in range(SL)]
    xm = []
    for s in range(SL):
        kept = jnp.logical_or(chain_i == labels[s], labels[s] == chains)
        xm.append(jnp.where(kept, xn[s * I : (s + 1) * I], 0.0).astype(BF16))
    xn = xn.astype(BF16)
    wsrc_t = wsrc_ref[...]
    for s in range(SL):
        lsend[s] = dot_nt(wsrc_t, xm[s]).astype(BF16)
    wt = wtgt_ref[...].astype(F32)
    wt = jnp.concatenate([wt] * (128 // PW), axis=0)
    wt_row = lax.broadcasted_iota(jnp.int32, wt.shape, 0) // PW
    packed = None
    for half in range(halves):
        for s in range(SL):
            k = half * SL + s
            rows = xm[s].reshape(Q, halves, 16, CH)[:, half].reshape(Q * 16, CH)
            part = dot_nt(rows, jnp.where(wt_row == k, wt, 0.0).astype(BF16))
            packed = part if packed is None else packed + part
    rsend[...] = packed.astype(BF16).reshape(Q, 16, 128)

    pl.semaphore_wait(barrier, n - 1)

    def copy_l(k):
        t = lax.rem(r + k, R)
        return pltpu.make_async_remote_copy(
            src_ref=lsend, dst_ref=lall.at[r], send_sem=l_send.at[k], recv_sem=l_recv.at[k],
            device_id=(g, t, c), device_id_type=MESH,
        )

    def copy_r(q, cc):
        return pltpu.make_async_remote_copy(
            src_ref=rsend.at[q], dst_ref=rall.at[r], send_sem=r_send.at[q * C + cc],
            recv_sem=r_recv.at[r], device_id=(g, c * Q + q, cc), device_id_type=MESH,
        )

    def copy_x(k):
        return pltpu.make_async_remote_copy(
            src_ref=x_ref, dst_ref=xall.at[c], send_sem=x_send.at[k], recv_sem=x_recv.at[k],
            device_id=(g, r, lax.rem(c + k, C)), device_id_type=MESH,
        )

    for q in range(Q):
        for cc in range(C):
            @pl.when(jnp.logical_not(jnp.logical_and(c * Q + q == r, cc == c)))
            def _(q=q, cc=cc):
                copy_r(q, cc).start()
    for k in range(1, R):
        copy_l(k).start()
    for k in range(1, C):
        copy_x(k).start()

    lall[r] = lsend[...]
    xall[c] = x_ref[...]
    own = lax.div(r, Q) == c

    @pl.when(own)
    def _():
        rall[r] = rsend[lax.rem(r, Q)]

    qt = dot_nt(transposed(wq_ref[...]), xn).astype(BF16)
    gate = jax.nn.sigmoid(dot_nt(transposed(wg_ref[...]), xn))
    row_block = lax.broadcasted_iota(jnp.int32, (128, I), 0) // D
    for s in range(SL):
        gt[s] = gate[:, s * I : (s + 1) * I]
        for h in range(H):
            base = (h // group) * 128
            piece = qt[base : base + 128, s * I : (s + 1) * I].astype(F32)
            qbd[s * H + h] = jnp.where(row_block == h % group, piece, 0.0).astype(BF16)
    for k in range(PW):
        piece = wfin_ref[k * PW : (k + 1) * PW, :]
        for m in range(128 // PW):
            wd[k // 2, m * PW : (m + 1) * PW, (k % 2) * Z : (k % 2 + 1) * Z] = piece
    cf[...] = couple_ref[...].astype(F32).reshape(I * J, Z)
    woff = woff_ref[...]
    w1 = woff.astype(BF16).astype(F32)
    w2 = (woff - w1).astype(BF16).astype(F32)
    w3 = (woff - w1 - w2).astype(BF16).astype(F32)
    woff_t = jnp.concatenate([w1, w2, w3, jnp.zeros_like(w1)], axis=0).astype(BF16)

    members = []
    for k in range(chains + 1):
        total = (label_ref[0] == k).astype(jnp.int32)
        for s in range(1, S):
            total = total + (label_ref[s] == k).astype(jnp.int32)
        members.append(total)

    for k in range(R):
        @pl.when(jnp.logical_not(jnp.logical_and(own, r == k)))
        def _(k=k):
            pltpu.make_async_remote_copy(
                src_ref=rsend.at[0], dst_ref=rall.at[k], send_sem=r_send.at[0],
                recv_sem=r_recv.at[k], device_id=(g, r, c), device_id_type=MESH,
            ).wait_recv()
    lane = lax.broadcasted_iota(jnp.int32, (16, 128), 1) // PW
    for k in range(R):
        tile = rall[k].astype(F32)
        for half in range(halves):
            for s in range(SL):
                rscr[pl.ds(half * 16 * S + k * SL + s, 16, stride=S), :] = jnp.where(
                    lane == half * SL + s, tile, 0.0
                )
    right = rscr[...].astype(BF16)

    def spread_right(cp, carry):
        res = dot_nn(right, wd[cp]).astype(BF16)
        for j in range(J):
            for e in range(2):
                bscr[
                    j // 2,
                    pl.ds(pl.multiple_of((2 * cp + e) * S, 16), S),
                    (j % 2) * Z : (j % 2 + 1) * Z,
                ] = res[j * S : (j + 1) * S, e * Z : (e + 1) * Z]
        return carry

    lax.fori_loop(0, PW // 2, spread_right, 0, unroll=UB)

    for k in range(1, R):
        copy_l(k).wait_recv()
    for k in range(R):
        for s in range(SL):
            piece = lall[k, s].astype(F32)
            for b in range(I // 128):
                at = pl.ds(b * PW * S + k * SL + s, PW, stride=S)
                lscr[at, :] = piece[:, b * 128 : (b + 1) * 128]
    left = jnp.concatenate(
        [lscr[b * PW * S : (b + 1) * PW * S, :].T for b in range(I // 128)], axis=0
    ).astype(BF16)

    chain_z = chain_i[:, :Z]

    def pair_step(jj, carry):
        update = dot_nn(left, bscr[jj])
        normed = []
        for e in range(2):
            j = 2 * jj + e
            chain_j = chain_of(r * J + j, start_ref, chains)
            own_rows = members[0]
            for k in range(1, chains):
                own_rows = jnp.where(chain_j == k, members[k], own_rows)
            same = 1.0 / (jnp.full((1, Z), members[chains] + own_rows, jnp.int32).astype(F32) + 0.001)
            other = 1.0 / (jnp.full((1, Z), members[chains], jnp.int32).astype(F32) + 0.001)
            factor = jnp.where(chain_z == chain_j, same, other)
            at = pl.ds(j, I, stride=J)
            state = (cf[at, :] + update[:, e * Z : (e + 1) * Z] * factor).astype(BF16).astype(F32)
            cf[at, :] = state
            normed.append(standardize(state).astype(BF16))
        res = dot_nt(woff_t, jnp.concatenate(normed, axis=0))
        res = res[:H] + res[H : 2 * H] + res[2 * H : 3 * H]
        for e in range(2):
            for b in range(I // 128):
                at = pl.ds(b * H * 16 + lax.rem(2 * jj, 16) + e, H, stride=16)
                biasf[at, :] = res[:, e * I + b * 128 : e * I + (b + 1) * 128]
        return carry

    ZC = R // 2
    z, core = lax.div(r, 2), lax.rem(r, 2)
    sibling = 2 * z + 1 - core

    def copy_b(half, k):
        return pltpu.make_async_remote_copy(
            src_ref=ball.at[r, half], dst_ref=ball.at[r, half],
            send_sem=b_send.at[half, k], recv_sem=b_recv.at[half, k],
            device_id=(g, 2 * lax.rem(z + k, ZC) + core, c), device_id_type=MESH,
        )

    def copy_f(half, k):
        slot = 2 * lax.rem(z + ZC - k, ZC) + core
        return pltpu.make_async_remote_copy(
            src_ref=ball.at[slot, half], dst_ref=ball.at[slot, half],
            send_sem=f_send.at[half, k], recv_sem=f_recv.at[half, k],
            device_id=(g, sibling, c), device_id_type=MESH,
        )

    for half in range(halves):
        lax.fori_loop(half * 8, half * 8 + 8, pair_step, 0, unroll=UP)
        for b in range(I // 128):
            ball[r, half, :, :, b * 128 : (b + 1) * 128] = (
                biasf[b * H * 16 : (b + 1) * H * 16, :].astype(BF16).reshape(H, 16, 128)
            )
        for k in range(1, ZC):
            copy_b(half, k).start()
        copy_f(half, 0).start()

    def forward(half):
        for k in range(1, ZC):
            copy_b(half, k).wait_recv()
            copy_f(half, k).start()

    for half in range(halves - 1):
        forward(half)

    pair_ref[...] = cf[...].astype(BF16).reshape(I, J, Z)

    for k in range(1, C):
        copy_x(k).wait_recv()
    wv_t = transposed(wkv_ref[:, inner:])
    for cc in range(C):
        block = standardize(xall[cc].astype(F32).reshape(SL * I, CH)).astype(BF16)
        keys = dot_nn(block, wkv_ref[:, :inner]).astype(BF16)
        vals = dot_nt(wv_t, block).astype(BF16)
        for s in range(SL):
            kscr[s, cc * I : (cc + 1) * I, :] = keys[s * I : (s + 1) * I]
            vt[s, :, cc * I : (cc + 1) * I] = vals[:, s * I : (s + 1) * I]
    chain_a = chain_of(lax.broadcasted_iota(jnp.int32, (A, I), 0), start_ref, chains)
    for s in range(SL):
        kept = jnp.logical_or(chain_a == labels[s], labels[s] == chains)
        madd[s] = jnp.where(kept, 0.0, -1000000000.0)

    scale = 1.0 / math.sqrt(D)

    def score(step, carry):
        s, h = lax.div(step, H), lax.rem(step, H)
        at = pl.ds(pl.multiple_of(lax.div(h, group) * 128, 128), 128)
        held[step] = dot_nn(kscr[s, :, at], qbd[step]) * scale + madd[s]
        return carry

    lax.fori_loop(0, SL * H, score, 0, unroll=US)
    forward(halves - 1)
    for half in range(halves):
        for k in range(ZC):
            copy_f(half, k).wait_recv()

    def attend(step, carry):
        s, h = lax.div(step, H), lax.rem(step, H)
        scores = held[step] + ball[:, :, h].astype(F32).reshape(A, I)
        weights = jnp.exp(scores - jnp.max(scores, axis=0, keepdims=True))
        total = jnp.sum(weights, axis=0, keepdims=True)
        rows = pl.ds(pl.multiple_of(h * D, D), D)
        attended = dot_nn(vt[s, rows, :], weights.astype(BF16)) / total
        gated[s, rows, :] = (gt[s, rows, :] * attended).astype(BF16)
        return carry

    lax.fori_loop(0, SL * H, attend, 0, unroll=UA)

    for s in range(SL):
        merged = dot_nn(transposed(gated[s]), wm_ref[...])
        out_ref[s] = (x_ref[s].astype(F32) + merged).astype(BF16)

    for q in range(Q):
        for cc in range(C):
            @pl.when(jnp.logical_not(jnp.logical_and(c * Q + q == r, cc == c)))
            def _(q=q, cc=cc):
                copy_r(q, cc).wait_send()
    for k in range(1, R):
        copy_l(k).wait_send()
    for k in range(1, C):
        copy_x(k).wait_send()
    for half in range(halves):
        for k in range(1, ZC):
            copy_b(half, k).wait_send()
        for k in range(ZC):
            copy_f(half, k).wait_send()


def per_device(R, C, homolog, couple, starts, labels, *weights):
    SL, I, CH = homolog.shape
    J, Z = couple.shape[1], couple.shape[2]
    S = labels.shape[0]
    wsrc, wtgt, wfin, woff, wq = weights[:5]
    PW, H, inner = wsrc.shape[1], woff.shape[1], wq.shape[1]
    A = C * I
    Q = I // J
    vmem = pl.BlockSpec(memory_space=pltpu.VMEM)
    smem = pl.BlockSpec(memory_space=pltpu.SMEM)
    dma = pltpu.SemaphoreType.DMA
    return pl.pallas_call(
        functools.partial(kernel, R, C),
        out_shape=(
            jax.ShapeDtypeStruct(homolog.shape, BF16),
            jax.ShapeDtypeStruct(couple.shape, BF16),
        ),
        in_specs=[smem, smem] + [vmem] * 10,
        out_specs=(vmem, vmem),
        scratch_shapes=[
            pltpu.VMEM((SL, PW, I), BF16),
            pltpu.VMEM((R, SL, PW, I), BF16),
            pltpu.VMEM((Q, 16, 128), BF16),
            pltpu.VMEM((R, 16, 128), BF16),
            pltpu.VMEM((C, SL, I, CH), BF16),
            pltpu.VMEM((I // 128 * PW * S, 128), F32),
            pltpu.VMEM((J * S, 128), F32),
            pltpu.VMEM((PW // 2, 128, 2 * Z), BF16),
            pltpu.VMEM((J // 2, PW * S, 2 * Z), BF16),
            pltpu.VMEM((I * J, Z), F32),
            pltpu.VMEM((I // 128 * H * 16, 128), F32),
            pltpu.VMEM((R, J // 16, H, 16, I), BF16),
            pltpu.VMEM((SL * H, 128, I), BF16),
            pltpu.VMEM((SL, inner, I), F32),
            pltpu.VMEM((SL, A, inner), BF16),
            pltpu.VMEM((SL, inner, A), BF16),
            pltpu.VMEM((SL, A, I), F32),
            pltpu.VMEM((SL, inner, I), BF16),
            pltpu.VMEM((SL * H, A, I), F32),
            dma((R,)), dma((R,)), dma((R,)), dma((R,)), dma((C,)), dma((C,)),
            *[dma((J // 16, R // 2))] * 4,
        ],
        compiler_params=pltpu.CompilerParams(
            collective_id=0, has_side_effects=True, vmem_limit_bytes=61 * 2**20
        ),
    )(starts, labels, homolog, couple, wsrc.T, wtgt.T, wfin, woff.T, *weights[4:])


def solution(mesh):
    spec = (
        P(("groups", "row"), "col", None),
        P(("groups", "col"), "row", None),
    )
    return jax.shard_map(
        functools.partial(per_device, mesh.shape["row"], mesh.shape["col"]),
        mesh=mesh,
        in_specs=spec + (P("groups"), P("groups")) + (P(),) * 8,
        out_specs=spec,
        check_vma=False,
    )
```
